32 devices in a mesh: table: 8 (over z, x), sub: 4 (over y, core).
Axes of the slice: x: 2, y: 2, z: 4, core: 2. Of those that a mesh axis runs over, the one named last changes fastest.
Arguments:
- pooled: bfloat16 [96, 8, 4, 32, 128], P('table', None, 'sub'), may hold values from -6 to 6
- field_owner: int32 [48], replicated, may hold values from 0 to 7, as said below
- w_squeeze: float32 [16, 48], replicated, may hold values from -2.5 to 2.5
- w_excite: float32 [1536, 16], replicated, may hold values from -1.5 to 1.5
- w_bilinear: float32 [32, 32], replicated, may hold values from -1 to 1
- tower_weight: bfloat16 [36096, 1024], P(('table', 'sub')), may hold values from -0.1875 to 0.1875
- tower_cotangent: bfloat16 [1024, 4096], P(None, ('table', 'sub')), may hold values from -6 to 6
Outputs:
- row_grads: bfloat16 [96, 8, 4, 32, 128], P('table', None, 'sub')
- tower_weight_grad: float32 [36096, 1024], P(('table', 'sub'))
- squeeze_grad: float32 [16, 48], replicated
- excite_grad: float32 [1536, 16], replicated
- bilinear_grad: float32 [32, 32], replicated
The draws below stay inside these ranges and needn't reach their ends.
Inputs may be any that keep to these rules, and one draw needn't show every extreme that they name: `field_owner`: each table index holds at most 12 fields, and some index holds exactly 12.
All inputs are finite; a program needn't handle non-finite values.
Results may differ from the reference program's by a relative error of at most 0.0074.
Values may be sent and summed in bfloat16 or wider, within the bound.
A program may use at most 192 MiB of HBM per device.

```python
import jax
import jax.numpy as jnp
from jax import lax

F = 48
E = 32
R = 16
H = 1024
B_DEV = 128
FSLOT = 12
SLOTS = 96
K = 36096
BATCH = 4096
N_TABLE = 8
N_SUB = 4


def draw_field_owner(key, part):
    first_key, order_key, shuffle_key = jax.random.split(jax.random.fold_in(key, 17), 3)
    capacity = N_TABLE * FSLOT
    favoured = jax.random.randint(first_key, (), 0, N_TABLE)
    positions = jnp.arange(capacity, dtype=jnp.int32)
    holders = positions // FSLOT
    scores = jax.random.permutation(order_key, capacity).astype(jnp.int32)
    scores = scores + jnp.where(holders == favoured, 0, capacity).astype(jnp.int32)
    ranked = jnp.argsort(scores, stable=True)
    chosen = ranked[:F] // FSLOT
    mixing = jax.random.permutation(shuffle_key, F)
    return chosen[mixing].astype(jnp.int32)


def levels(rng, shape, cuts, low, top_value):
    def one(dim, parts):
        steps = jax.random.uniform(jax.random.fold_in(jax.random.fold_in(rng, 6), dim), (parts,), jnp.float32, low / len(cuts), top_value / len(cuts))
        return jnp.repeat(jnp.exp(steps), shape[dim] // parts).reshape((-1,) + (1,) * (len(shape) - dim - 1))

    factor_of = one(*cuts[0])
    for cut in cuts[1:]:
        factor_of = factor_of * one(*cut)
    return factor_of


def bell_draw(key, extent, scale, limit, cuts=(), kind=jnp.bfloat16):
    gain = levels(key, extent, cuts, -0.22, 0.18) if cuts else 1.0
    drawn = jax.random.normal(key, extent, jnp.float32) * scale * gain
    return jnp.minimum(jnp.maximum(drawn, -limit), limit).astype(kind)


def setup_inputs(seed: int = 0) -> dict:
    streams_of = jax.random.split(jax.random.key(seed), 8)
    pooled = bell_draw(streams_of[0], (SLOTS, N_TABLE, N_SUB, E, B_DEV), 1.0, 6.0, ((0, 8), (2, 4)))
    field_owner = draw_field_owner(jax.random.fold_in(streams_of[7], 71), 0)
    w_squeeze = bell_draw(streams_of[2], (R, F), (F // 8) ** -0.5, 2.5, (), jnp.float32)
    w_excite = bell_draw(streams_of[3], (F * E, R), R ** -0.5, 1.5, (), jnp.float32)
    w_bilinear = bell_draw(streams_of[4], (E, E), E ** -0.5, 1.0, (), jnp.float32)
    tower_weight = bell_draw(streams_of[5], (K, H), H ** -0.5, 0.1875, ((0, 32),))
    tower_cotangent = bell_draw(streams_of[6], (H, BATCH), 1.0, 6.0, ((1, 32),))
    return dict(pooled=pooled, field_owner=field_owner, w_squeeze=w_squeeze, w_excite=w_excite, w_bilinear=w_bilinear, tower_weight=tower_weight, tower_cotangent=tower_cotangent)


def hadamard_table(width):
    index = jnp.arange(width, dtype=jnp.int32)
    both = index[:, None] & index[None, :]
    parity = jnp.zeros((width, width), jnp.int32)
    for bit_pos in range(width.bit_length()):
        parity = parity ^ both >> bit_pos & 1
    return (1 - 2 * parity).astype(jnp.float32)

def slot_table(field_owner, per_owner):
    count = field_owner.shape[0]
    order = jnp.arange(count, dtype=jnp.int32)
    same = field_owner[:, None] == field_owner[None, :]
    earlier = order[:, None] > order[None, :]
    position = lax.optimization_barrier(jnp.sum((same & earlier).astype(jnp.int32), axis=1))
    return (field_owner * per_owner + position).astype(jnp.int32)

def forward(fields, w_squeeze, w_excite, w_bilinear):
    count, width, samples = fields.shape
    high = lax.Precision.HIGHEST
    squeezed = lax.optimization_barrier(jnp.mean(fields, axis=1))
    activated = jax.nn.silu(jnp.dot(w_squeeze, squeezed, precision=high))
    excite = jnp.dot(w_excite, activated, precision=high).reshape(count, width, samples)
    weighted = fields * (1.0 + excite)
    mapped = jnp.einsum('ed,fen->fdn', w_bilinear, weighted, precision=high)
    pieces = [mapped[left][None] * weighted[left + 1:] for left in range(count - 1)]
    pairs = jnp.concatenate(pieces, axis=0)
    return pairs.reshape(-1, samples).astype(jnp.bfloat16)

def reference(pooled, field_owner, w_squeeze, w_excite, w_bilinear, tower_weight, tower_cotangent):
    groups = N_TABLE * N_SUB
    scale = 1.0 / E ** 0.5
    signs = hadamard_table(E)
    rotated = (jnp.einsum('ij,ktsjb->ktsib', signs, pooled.astype(jnp.float32)) * scale).astype(jnp.bfloat16)
    slot_index = slot_table(field_owner, FSLOT)
    chosen = jnp.take(rotated, slot_index, axis=0)
    chosen = jnp.transpose(chosen, (1, 2, 0, 3, 4)).reshape(groups, F, E, B_DEV)
    cotangent = jnp.transpose(tower_cotangent.reshape(H, groups, B_DEV), (1, 0, 2))

    def one_block(carry, inputs):
        weight_total, g_squeeze, g_excite, g_bilinear = carry
        block, grad_in = inputs
        fields = jnp.einsum('ij,fjn->fin', signs, block.astype(jnp.float32)) * scale
        pairs, back = jax.vjp(forward, fields, w_squeeze, w_excite, w_bilinear)
        weight_total = weight_total + jnp.dot(pairs, grad_in.T, preferred_element_type=jnp.float32)
        pair_grad = jnp.dot(tower_weight, grad_in, preferred_element_type=jnp.float32).astype(jnp.bfloat16)
        field_grad, d_squeeze, d_excite, d_bilinear = back(pair_grad)
        carry = (weight_total, g_squeeze + d_squeeze, g_excite + d_excite, g_bilinear + d_bilinear)
        return (carry, field_grad.astype(jnp.bfloat16))
    start = (jnp.zeros((K, H), jnp.float32), jnp.zeros((R, F), jnp.float32), jnp.zeros((F * E, R), jnp.float32), jnp.zeros((E, E), jnp.float32))
    totals, field_grads = lax.scan(one_block, start, (chosen, cotangent))
    onehot = (slot_index[None, :] == jnp.arange(SLOTS, dtype=jnp.int32)[:, None]).astype(jnp.float32)
    placed = jnp.einsum('sf,gfen->gsen', onehot, field_grads.astype(jnp.float32)).astype(jnp.bfloat16)
    placed = placed.reshape(N_TABLE, N_SUB, SLOTS, E, B_DEV)
    row_grads = jnp.transpose(placed, (2, 0, 1, 3, 4))
    inverse = 1.0 / BATCH
    return (row_grads, totals[0] * inverse, totals[1] * inverse, totals[2] * inverse, totals[3] * inverse)
```

```python
import functools

import jax
import jax.numpy as jnp
import numpy as np
from jax import lax
from jax.experimental import pallas as pl
from jax.experimental.pallas import tpu as pltpu
from jax.sharding import Mesh
from jax.sharding import PartitionSpec as P

HIGH = lax.Precision.HIGHEST
TABLE = ("a", "l")
GROUP = ("l", "sub")
EVERY = ("a", "l", "sub")


def hadamard_table(width):
    index = jnp.arange(width, dtype=jnp.int32)
    both = index[:, None] & index[None, :]
    parity = jnp.zeros((width, width), jnp.int32)
    for bit_pos in range(width.bit_length()):
        parity = parity ^ both >> bit_pos & 1
    return (1 - 2 * parity).astype(jnp.bfloat16)


def slot_table(field_owner, per_owner):
    count = field_owner.shape[0]
    order = jnp.arange(count, dtype=jnp.int32)
    same = field_owner[:, None] == field_owner[None, :]
    earlier = order[:, None] > order[None, :]
    position = jnp.sum((same & earlier).astype(jnp.int32), axis=1)
    return field_owner * per_owner + position


def bits_of(size):
    return [1 << k for k in range(size.bit_length() - 1)]


def swap(x, size, bit):
    return lax.ppermute(x, GROUP, [(d, d ^ bit) for d in range(size)])


def gather_rows(shard, size, me):
    held = shard[None]
    offsets = [0]
    for bit in reversed(bits_of(size)):
        held = jnp.concatenate([held, swap(held, size, bit)], axis=0)
        offsets = offsets + [o ^ bit for o in offsets]
    place = np.argsort(np.array(offsets))
    order = jnp.asarray(place, jnp.int32)[jnp.arange(size, dtype=jnp.int32) ^ me]
    parts = [lax.dynamic_index_in_dim(held, order[d], 0, keepdims=False) for d in range(size)]
    return jnp.concatenate(parts, axis=0)


def scatter_rows(total, size, me):
    held = total.reshape(size, total.shape[0] // size, total.shape[1])
    result = None
    for bit in bits_of(size):
        half = held.shape[0] // 2
        view = held.reshape(half, 2, held.shape[1], held.shape[2])
        side = lax.rem(me // bit, 2)
        keep = lax.dynamic_index_in_dim(view, side, 1, keepdims=False)
        give = lax.dynamic_index_in_dim(view, 1 - side, 1, keepdims=False)
        got = swap(give, size, bit)
        result = keep.astype(jnp.float32) + got.astype(jnp.float32)
        held = result.astype(jnp.bfloat16)
    return result[0] if result is not None else held[0].astype(jnp.float32)


def tower_kernel(
    chunk, left_ref, right_ref, w_ref, cot_ref, wt_ref, fwd_ref, bwd_ref,
    twg_ref, dwt_ref, gb_ref, cot2, mf, dm, dw, pg, prs,
):
    parts, count, width, lanes = wt_ref.shape
    step = pl.program_id(0)
    depth = cot2.shape[0]
    tile = min(256, depth)
    ntile = min(256, parts * lanes)

    def columns(a):
        return slice(a * lanes, (a + 1) * lanes)

    @pl.when(step == 0)
    def _():
        for a in range(parts):
            cot2[:, columns(a)] = cot_ref[a]

        @pl.loop(0, count)
        def _(f):
            rows = jnp.concatenate([wt_ref[a, f] for a in range(parts)], axis=1)
            both = jnp.dot(fwd_ref[...], rows, preferred_element_type=jnp.float32)
            value = both[:width] + both[width:]
            for a in range(parts):
                mf[a, f] = value[:, columns(a)]
                dm[a, f] = jnp.zeros((width, lanes), jnp.float32)
                dw[a, f] = jnp.zeros((width, lanes), jnp.float32)

    @pl.loop(0, parts * lanes // ntile)
    def _(c):
        cols = pl.ds(pl.multiple_of(c * ntile, ntile), ntile)
        pg[:, cols] = jnp.dot(w_ref[...], cot2[:, cols], preferred_element_type=jnp.float32)

    @pl.loop(0, chunk)
    def _(q):
        i = left_ref[step * chunk + q]
        j = right_ref[step * chunk + q]
        rows = pl.ds(pl.multiple_of(q * width, width), width)
        for a in range(parts):
            g = pg[rows, columns(a)]
            w = wt_ref[a, j].astype(jnp.float32)
            m = mf[a, i]
            prs[rows, columns(a)] = (m * w).astype(jnp.bfloat16)
            dm[a, i] += g * w
            dw[a, j] += g * m

    @pl.loop(0, depth // tile)
    def _(c):
        cols = pl.ds(pl.multiple_of(c * tile, tile), tile)
        twg_ref[:, cols] = lax.dot_general(
            prs[...], cot2[cols, :], (((1,), (1,)), ((), ())), preferred_element_type=jnp.float32
        ).astype(jnp.bfloat16)

    @pl.when(step == pl.num_programs(0) - 1)
    def _():
        gb_ref[...] = jnp.zeros_like(gb_ref)

        @pl.loop(0, count)
        def _(f):
            d = jnp.concatenate([dm[a, f].astype(jnp.bfloat16) for a in range(parts)], axis=1)
            rows = jnp.concatenate([wt_ref[a, f] for a in range(parts)], axis=1)
            both = jnp.dot(bwd_ref[...], d, preferred_element_type=jnp.float32)
            value = both[:width] + both[width:]
            for a in range(parts):
                dwt_ref[a, f] = (dw[a, f] + value[:, columns(a)]).astype(jnp.bfloat16)
            gb_ref[...] += lax.dot_general(
                rows, d, (((1,), (1,)), ((), ())), preferred_element_type=jnp.float32
            )


def two_parts(matrix):
    top = matrix.astype(jnp.bfloat16)
    rest = (matrix - top.astype(jnp.float32)).astype(jnp.bfloat16)
    return jnp.concatenate([top, rest], axis=0)


def tower_step(left, right, weights, cot, weighted, w_bilinear):
    parts, count, width, lanes = weighted.shape
    depth = cot.shape[1]
    pairs = left.shape[0]
    steps = next(c for c in (3, 2, 4, 5, 6, 7, 1) if pairs % c == 0)
    chunk = pairs // steps
    rows = chunk * width
    samples = parts * lanes

    def whole(shape):
        return pl.BlockSpec(shape, lambda s, *_: (0,) * len(shape), pipeline_mode=pl.Buffered(1))

    big = (parts, count, width, lanes)
    return pl.pallas_call(
        functools.partial(tower_kernel, chunk),
        grid_spec=pltpu.PrefetchScalarGridSpec(
            num_scalar_prefetch=2,
            grid=(steps,),
            in_specs=[
                pl.BlockSpec((rows, depth), lambda s, *_: (s, 0)),
                whole(cot.shape),
                whole(big),
                whole((2 * width, width)),
                whole((2 * width, width)),
            ],
            out_specs=[
                pl.BlockSpec((rows, depth), lambda s, *_: (s, 0)),
                whole(big),
                whole((width, width)),
            ],
            scratch_shapes=[
                pltpu.VMEM((depth, samples), jnp.bfloat16),
                pltpu.VMEM(big, jnp.float32),
                pltpu.VMEM(big, jnp.float32),
                pltpu.VMEM(big, jnp.float32),
                pltpu.VMEM((rows, samples), jnp.float32),
                pltpu.VMEM((rows, samples), jnp.bfloat16),
            ],
        ),
        out_shape=[
            jax.ShapeDtypeStruct((pairs * width, depth), jnp.bfloat16),
            jax.ShapeDtypeStruct(big, jnp.bfloat16),
            jax.ShapeDtypeStruct((width, width), jnp.float32),
        ],
        compiler_params=pltpu.CompilerParams(
            dimension_semantics=("arbitrary",), vmem_limit_bytes=60 * 1024 * 1024
        ),
        cost_estimate=pl.CostEstimate(
            flops=4 * pairs * width * depth * samples,
            bytes_accessed=4 * pairs * width * depth,
            transcendentals=0,
        ),
    )(left, right, weights, cot, weighted, two_parts(w_bilinear.T), two_parts(w_bilinear))


def on_device(pooled, field_owner, w_squeeze, w_excite, w_bilinear, tower_weight, tower_cotangent):
    per_owner, width, samples = pooled.shape[0], pooled.shape[3], pooled.shape[4]
    count = field_owner.shape[0]
    hidden = w_squeeze.shape[0]
    parts, locals_, subs = lax.axis_size("a"), lax.axis_size("l"), lax.axis_size("sub")
    tables = parts * locals_
    size = locals_ * subs
    me = lax.axis_index("l") * subs + lax.axis_index("sub")
    scale = 1.0 / width**0.5
    signs = hadamard_table(width)

    weights = gather_rows(tower_weight, size, me)
    cot = lax.all_gather(tower_cotangent, "a", axis=0, tiled=False)

    rotated = (
        jnp.einsum("ij,ktsjb->ktsib", signs, pooled, preferred_element_type=jnp.float32) * scale
    ).astype(jnp.bfloat16)
    received = lax.all_to_all(rotated, TABLE, split_axis=1, concat_axis=0, tiled=True)
    received = received.reshape(per_owner * tables, width, samples)
    slot_index = slot_table(field_owner, per_owner)
    selected = jnp.take(received, slot_index, axis=0)
    fields = jnp.einsum("ij,fjn->fin", signs, selected, preferred_element_type=jnp.float32) * scale
    squeezed = jnp.mean(fields, axis=1)
    raw = jnp.dot(w_squeeze, squeezed, precision=HIGH)
    gate = jax.nn.sigmoid(raw)
    activated = raw * gate
    excite = jnp.dot(w_excite, activated, precision=HIGH).reshape(count, width, samples)
    weighted = fields * (1.0 + excite)
    weighted_all = lax.all_gather(weighted.astype(jnp.bfloat16), "a", axis=0, tiled=False)

    table_left, table_right = np.triu_indices(count, 1)
    mine = table_left.shape[0] // parts
    start = lax.axis_index("a") * mine
    left = lax.dynamic_slice_in_dim(jnp.asarray(table_left, jnp.int32), start, mine)
    right = lax.dynamic_slice_in_dim(jnp.asarray(table_right, jnp.int32), start, mine)
    totals, partial, d_bilinear = tower_step(left, right, weights, cot, weighted_all, w_bilinear)

    arrived = lax.all_to_all(partial, "a", split_axis=0, concat_axis=0, tiled=True)
    d_weighted = jnp.sum(arrived.astype(jnp.float32), axis=0)
    weight_total = scatter_rows(totals, size, me)

    d_excite = (d_weighted * fields).reshape(count * width, samples)
    g_excite = lax.dot_general(activated, d_excite, (((1,), (1,)), ((), ())), precision=HIGH)
    d_act = lax.dot_general(w_excite, d_excite, (((0,), (0,)), ((), ())), precision=HIGH)
    d_raw = d_act * (gate * (1.0 + raw * (1.0 - gate)))
    g_squeeze = lax.dot_general(d_raw, squeezed, (((1,), (1,)), ((), ())), precision=HIGH)
    d_squeezed = lax.dot_general(w_squeeze, d_raw, (((0,), (0,)), ((), ())), precision=HIGH)
    field_grad = d_weighted * (1.0 + excite) + (d_squeezed * (1.0 / width))[:, None, :]

    flat = jnp.concatenate([g_excite.reshape(-1), g_squeeze.reshape(-1), d_bilinear.reshape(-1)])
    flat = jnp.pad(flat, (0, -flat.shape[0] % 1024)).reshape(-1, 128)
    inverse = 1.0 / (tables * subs * samples)
    flat = (lax.psum(flat, EVERY) * inverse).reshape(-1)
    n_excite, n_squeeze = count * width * hidden, hidden * count
    g_excite = flat[:n_excite].reshape(hidden, count * width).T
    g_squeeze = flat[n_excite : n_excite + n_squeeze].reshape(hidden, count)
    at = n_excite + n_squeeze
    g_bilinear = flat[at : at + width * width].reshape(width, width)

    slot_count = per_owner * tables
    onehot = (slot_index[None, :] == jnp.arange(slot_count, dtype=jnp.int32)[:, None]).astype(
        jnp.bfloat16
    )
    placed = jnp.einsum(
        "sf,fen->sen", onehot, field_grad.astype(jnp.bfloat16), preferred_element_type=jnp.float32
    ).astype(jnp.bfloat16)
    placed = placed.reshape(slot_count, 1, 1, width, samples)
    row_grads = lax.all_to_all(placed, TABLE, split_axis=0, concat_axis=1, tiled=True)
    return (row_grads, weight_total * inverse, g_squeeze, g_excite, g_bilinear)


def solution(mesh):
    tables, subs = mesh.shape["table"], mesh.shape["sub"]

    def run(pooled, field_owner, *rest):
        count = field_owner.shape[0]
        pairs = count * (count - 1) // 2
        parts = max(a for a in range(1, tables + 1) if tables % a == 0 and pairs % a == 0)
        fine = Mesh(mesh.devices.reshape(parts, tables // parts, subs), EVERY)
        return jax.shard_map(
            on_device,
            mesh=fine,
            in_specs=(
                P(TABLE, None, "sub", None, None),
                P(),
                P(),
                P(),
                P(),
                P(EVERY, None),
                P(None, EVERY),
            ),
            out_specs=(P(TABLE, None, "sub", None, None), P(EVERY, None), P(), P(), P()),
            check_vma=False,
        )(pooled, field_owner, *rest)

    return run
```

```python
import functools

import jax
import jax.numpy as jnp
import numpy as np
from jax import lax
from jax.experimental import pallas as pl
from jax.experimental.pallas import tpu as pltpu
from jax.sharding import Mesh
from jax.sharding import PartitionSpec as P

HIGH = lax.Precision.HIGHEST
TABLE = ("a", "l")
GROUP = ("l", "sub")
EVERY = ("a", "l", "sub")


def hadamard_table(width):
    index = jnp.arange(width, dtype=jnp.int32)
    both = index[:, None] & index[None, :]
    parity = jnp.zeros((width, width), jnp.int32)
    for bit_pos in range(width.bit_length()):
        parity = parity ^ both >> bit_pos & 1
    return (1 - 2 * parity).astype(jnp.bfloat16)


def slot_table(field_owner, per_owner):
    count = field_owner.shape[0]
    order = jnp.arange(count, dtype=jnp.int32)
    same = field_owner[:, None] == field_owner[None, :]
    earlier = order[:, None] > order[None, :]
    position = jnp.sum((same & earlier).astype(jnp.int32), axis=1)
    return field_owner * per_owner + position


def bits_of(size):
    return [1 << k for k in range(size.bit_length() - 1)]


def swap(x, size, bit):
    return lax.ppermute(x, GROUP, [(d, d ^ bit) for d in range(size)])


def spread(own, axis, size, after=None):
    held = {0: own}
    for bit in reversed(bits_of(size)):
        pairs = [(d, d ^ bit) for d in range(size)]
        for offset in list(held):
            block = held[offset]
            if offset and after is not None:
                block = lax.optimization_barrier((block, after))[0]
            held[offset ^ bit] = lax.ppermute(block, axis, pairs)
    return [held[r] for r in range(size)]


def scatter_rows(total, size, me):
    held = total.reshape(size, total.shape[0] // size, total.shape[1])
    result = None
    for bit in bits_of(size):
        half = held.shape[0] // 2
        view = held.reshape(half, 2, held.shape[1], held.shape[2])
        side = lax.rem(me // bit, 2)
        keep = lax.dynamic_index_in_dim(view, side, 1, keepdims=False)
        give = lax.dynamic_index_in_dim(view, 1 - side, 1, keepdims=False)
        got = swap(give, size, bit)
        result = keep.astype(jnp.float32) + got.astype(jnp.float32)
        held = result.astype(jnp.bfloat16)
    return result[0] if result is not None else held[0].astype(jnp.float32)


def tower_kernel(
    chunk, left_ref, right_ref, order_ref, pg_ref, cot_ref, wt_ref, fwd_ref, bwd_ref,
    twg_ref, dwt_ref, gb_ref, mf, dm, dw, prs,
):
    parts, count, width, lanes = wt_ref.shape
    step = pl.program_id(0)
    depth = cot_ref.shape[0]
    tile = min(256, depth)
    order = [order_ref[a] for a in range(parts)]

    def columns(a):
        return slice(a * lanes, (a + 1) * lanes)

    @pl.when(step == 0)
    def _():
        @pl.loop(0, count)
        def _(f):
            rows = jnp.concatenate([wt_ref[order[a], f] for a in range(parts)], axis=1)
            both = jnp.dot(fwd_ref[...], rows, preferred_element_type=jnp.float32)
            value = both[:width] + both[width:]
            for a in range(parts):
                mf[a, f] = value[:, columns(a)]
                dm[a, f] = jnp.zeros((width, lanes), jnp.float32)
                dw[a, f] = jnp.zeros((width, lanes), jnp.float32)

    @pl.loop(0, chunk)
    def _(q):
        i = left_ref[step * chunk + q]
        j = right_ref[step * chunk + q]
        rows = pl.ds(pl.multiple_of(q * width, width), width)
        for a in range(parts):
            g = pg_ref[rows, columns(a)].astype(jnp.float32)
            w = wt_ref[order[a], j].astype(jnp.float32)
            m = mf[a, i]
            prs[rows, columns(a)] = (m * w).astype(jnp.bfloat16)
            dm[a, i] += g * w
            dw[a, j] += g * m

    @pl.loop(0, depth // tile)
    def _(c):
        cols = pl.ds(pl.multiple_of(c * tile, tile), tile)
        twg_ref[:, cols] = lax.dot_general(
            prs[...], cot_ref[cols, :], (((1,), (1,)), ((), ())), preferred_element_type=jnp.float32
        ).astype(jnp.bfloat16)

    @pl.when(step == pl.num_programs(0) - 1)
    def _():
        gb_ref[...] = jnp.zeros_like(gb_ref)

        @pl.loop(0, count)
        def _(f):
            d = jnp.concatenate([dm[a, f].astype(jnp.bfloat16) for a in range(parts)], axis=1)
            rows = jnp.concatenate([wt_ref[order[a], f] for a in range(parts)], axis=1)
            both = jnp.dot(bwd_ref[...], d, preferred_element_type=jnp.float32)
            value = both[:width] + both[width:]
            for a in range(parts):
                dwt_ref[order[a], f] = (dw[a, f] + value[:, columns(a)]).astype(jnp.bfloat16)
            gb_ref[...] += lax.dot_general(
                rows, d, (((1,), (1,)), ((), ())), preferred_element_type=jnp.float32
            )


def two_parts(matrix):
    top = matrix.astype(jnp.bfloat16)
    rest = (matrix - top.astype(jnp.float32)).astype(jnp.bfloat16)
    return jnp.concatenate([top, rest], axis=0)


def tower_step(left, right, order, pair_grad, cot, weighted, w_bilinear):
    parts, count, width, lanes = weighted.shape
    depth = cot.shape[0]
    pairs = left.shape[0]
    steps = next(c for c in (3, 2, 4, 5, 6, 7, 1) if pairs % c == 0)
    chunk = pairs // steps
    rows = chunk * width
    samples = parts * lanes

    def whole(shape):
        return pl.BlockSpec(shape, lambda s, *_: (0,) * len(shape), pipeline_mode=pl.Buffered(1))

    big = (parts, count, width, lanes)
    return pl.pallas_call(
        functools.partial(tower_kernel, chunk),
        grid_spec=pltpu.PrefetchScalarGridSpec(
            num_scalar_prefetch=3,
            grid=(steps,),
            in_specs=[
                pl.BlockSpec((rows, samples), lambda s, *_: (s, 0)),
                whole(cot.shape),
                whole(big),
                whole((2 * width, width)),
                whole((2 * width, width)),
            ],
            out_specs=[
                pl.BlockSpec((rows, depth), lambda s, *_: (s, 0)),
                whole(big),
                whole((width, width)),
            ],
            scratch_shapes=[
                pltpu.VMEM(big, jnp.float32),
                pltpu.VMEM(big, jnp.float32),
                pltpu.VMEM(big, jnp.float32),
                pltpu.VMEM((rows, samples), jnp.bfloat16),
            ],
        ),
        out_shape=[
            jax.ShapeDtypeStruct((pairs * width, depth), jnp.bfloat16),
            jax.ShapeDtypeStruct(big, jnp.bfloat16),
            jax.ShapeDtypeStruct((width, width), jnp.float32),
        ],
        compiler_params=pltpu.CompilerParams(
            dimension_semantics=("arbitrary",), vmem_limit_bytes=60 * 1024 * 1024
        ),
        cost_estimate=pl.CostEstimate(
            flops=2 * pairs * width * depth * samples,
            bytes_accessed=4 * pairs * width * depth,
            transcendentals=0,
        ),
    )(left, right, order, pair_grad, cot, weighted, two_parts(w_bilinear.T), two_parts(w_bilinear))


def on_device(pooled, field_owner, w_squeeze, w_excite, w_bilinear, tower_weight, tower_cotangent):
    per_owner, width, samples = pooled.shape[0], pooled.shape[3], pooled.shape[4]
    count = field_owner.shape[0]
    hidden = w_squeeze.shape[0]
    parts, locals_, subs = lax.axis_size("a"), lax.axis_size("l"), lax.axis_size("sub")
    tables = parts * locals_
    size = locals_ * subs
    me = lax.axis_index("l") * subs + lax.axis_index("sub")
    scale = 1.0 / width**0.5
    signs = hadamard_table(width)

    rotated = (
        jnp.einsum("ij,ktsjb->ktsib", signs, pooled, preferred_element_type=jnp.float32) * scale
    ).astype(jnp.bfloat16)
    received = lax.all_to_all(rotated, TABLE, split_axis=1, concat_axis=0, tiled=True)
    received = received.reshape(per_owner * tables, width, samples)
    slot_index = slot_table(field_owner, per_owner)
    selected = jnp.take(received, slot_index, axis=0)
    fields = jnp.einsum("ij,fjn->fin", signs, selected, preferred_element_type=jnp.float32) * scale
    squeezed = jnp.mean(fields, axis=1)
    raw = jnp.dot(w_squeeze, squeezed, precision=HIGH)
    gate = jax.nn.sigmoid(raw)
    activated = raw * gate
    excite = jnp.dot(w_excite, activated, precision=HIGH).reshape(count, width, samples)
    weighted = fields * (1.0 + excite)
    narrow = weighted.astype(jnp.bfloat16)
    weighted_all = lax.all_gather(narrow, "a", axis=0, tiled=False)

    mine_a = lax.axis_index("a")
    order = jnp.arange(parts, dtype=jnp.int32) ^ mine_a
    cot = jnp.concatenate(spread(tower_cotangent, "a", parts, narrow), axis=1)
    shards = spread(tower_weight, GROUP, size, narrow)
    rows = tower_weight.shape[0]
    pair_grad = jnp.zeros((size * rows, cot.shape[1]), jnp.bfloat16)
    for offset, shard in enumerate(shards):
        block = jnp.dot(shard, cot, preferred_element_type=jnp.float32).astype(jnp.bfloat16)
        pair_grad = lax.dynamic_update_slice_in_dim(pair_grad, block, (me ^ offset) * rows, 0)

    table_left, table_right = np.triu_indices(count, 1)
    mine = table_left.shape[0] // parts
    start = mine_a * mine
    left = lax.dynamic_slice_in_dim(jnp.asarray(table_left, jnp.int32), start, mine)
    right = lax.dynamic_slice_in_dim(jnp.asarray(table_right, jnp.int32), start, mine)
    totals, partial, d_bilinear = tower_step(
        left, right, order, pair_grad, cot, weighted_all, w_bilinear
    )

    arrived = lax.all_to_all(partial, "a", split_axis=0, concat_axis=0, tiled=True)
    d_weighted = jnp.sum(arrived.astype(jnp.float32), axis=0)
    weight_total = scatter_rows(totals, size, me)

    d_excite = (d_weighted * fields).reshape(count * width, samples)
    g_excite = lax.dot_general(activated, d_excite, (((1,), (1,)), ((), ())), precision=HIGH)
    d_act = lax.dot_general(w_excite, d_excite, (((0,), (0,)), ((), ())), precision=HIGH)
    d_raw = d_act * (gate * (1.0 + raw * (1.0 - gate)))
    g_squeeze = lax.dot_general(d_raw, squeezed, (((1,), (1,)), ((), ())), precision=HIGH)
    d_squeezed = lax.dot_general(w_squeeze, d_raw, (((0,), (0,)), ((), ())), precision=HIGH)
    field_grad = d_weighted * (1.0 + excite) + (d_squeezed * (1.0 / width))[:, None, :]

    flat = jnp.concatenate([g_excite.reshape(-1), g_squeeze.reshape(-1), d_bilinear.reshape(-1)])
    devices = tables * subs
    inverse = 1.0 / (devices * samples)
    flat = jnp.pad(flat, (0, -flat.shape[0] % (devices * 1024))).reshape(devices, -1, 128)
    share = jnp.sum(lax.all_to_all(flat, EVERY, 0, 0, tiled=True), axis=0) * inverse
    share = jnp.broadcast_to(share[None], flat.shape)
    flat = lax.all_to_all(share, EVERY, 0, 0, tiled=True).reshape(-1)
    n_excite, n_squeeze = count * width * hidden, hidden * count
    g_excite = flat[:n_excite].reshape(hidden, count * width).T
    g_squeeze = flat[n_excite : n_excite + n_squeeze].reshape(hidden, count)
    at = n_excite + n_squeeze
    g_bilinear = flat[at : at + width * width].reshape(width, width)

    slot_count = per_owner * tables
    onehot = (slot_index[None, :] == jnp.arange(slot_count, dtype=jnp.int32)[:, None]).astype(
        jnp.bfloat16
    )
    placed = jnp.einsum(
        "sf,fen->sen", onehot, field_grad.astype(jnp.bfloat16), preferred_element_type=jnp.float32
    ).astype(jnp.bfloat16)
    placed = placed.reshape(slot_count, 1, 1, width, samples)
    row_grads = lax.all_to_all(placed, TABLE, split_axis=0, concat_axis=1, tiled=True)
    return (row_grads, weight_total * inverse, g_squeeze, g_excite, g_bilinear)


def solution(mesh):
    tables, subs = mesh.shape["table"], mesh.shape["sub"]

    def run(pooled, field_owner, *rest):
        count = field_owner.shape[0]
        pairs = count * (count - 1) // 2
        parts = max(a for a in range(1, tables + 1) if tables % a == 0 and pairs % a == 0)
        fine = Mesh(mesh.devices.reshape(parts, tables // parts, subs), EVERY)
        return jax.shard_map(
            on_device,
            mesh=fine,
            in_specs=(
                P(TABLE, None, "sub", None, None),
                P(),
                P(),
                P(),
                P(),
                P(EVERY, None),
                P(None, EVERY),
            ),
            out_specs=(P(TABLE, None, "sub", None, None), P(EVERY, None), P(), P(), P()),
            check_vma=False,
        )(pooled, field_owner, *rest)

    return run
```

```python
import functools

import jax
import jax.numpy as jnp
import numpy as np
from jax import lax
from jax.experimental import pallas as pl
from jax.experimental.pallas import tpu as pltpu
from jax.sharding import Mesh
from jax.sharding import PartitionSpec as P

HIGH = lax.Precision.HIGHEST
TABLE = ("a", "l")
GROUP = ("l", "sub")
EVERY = ("a", "l", "sub")


def hadamard_table(width):
    index = jnp.arange(width, dtype=jnp.int32)
    both = index[:, None] & index[None, :]
    parity = jnp.zeros((width, width), jnp.int32)
    for bit_pos in range(width.bit_length()):
        parity = parity ^ both >> bit_pos & 1
    return (1 - 2 * parity).astype(jnp.bfloat16)


def slot_table(field_owner, per_owner):
    count = field_owner.shape[0]
    order = jnp.arange(count, dtype=jnp.int32)
    same = field_owner[:, None] == field_owner[None, :]
    earlier = order[:, None] > order[None, :]
    position = jnp.sum((same & earlier).astype(jnp.int32), axis=1)
    return field_owner * per_owner + position


def bits_of(size):
    return [1 << k for k in range(size.bit_length() - 1)]


def swap(x, size, bit):
    return lax.ppermute(x, GROUP, [(d, d ^ bit) for d in range(size)])


def spread(own, axis, size, after=None):
    held = {0: own}
    for bit in reversed(bits_of(size)):
        pairs = [(d, d ^ bit) for d in range(size)]
        for offset in list(held):
            block = held[offset]
            if offset and after is not None:
                block = lax.optimization_barrier((block, after))[0]
            held[offset ^ bit] = lax.ppermute(block, axis, pairs)
    return [held[r] for r in range(size)]


def scatter_rows(total, size, me):
    held = total.reshape(size, total.shape[0] // size, total.shape[1])
    result = None
    for bit in bits_of(size):
        half = held.shape[0] // 2
        view = held.reshape(half, 2, held.shape[1], held.shape[2])
        side = lax.rem(me // bit, 2)
        keep = lax.dynamic_index_in_dim(view, side, 1, keepdims=False)
        give = lax.dynamic_index_in_dim(view, 1 - side, 1, keepdims=False)
        got = swap(give, size, bit)
        result = keep.astype(jnp.float32) + got.astype(jnp.float32)
        held = result.astype(jnp.bfloat16)
    return result[0] if result is not None else held[0].astype(jnp.float32)


def tower_kernel(
    chunk, left_ref, right_ref, order_ref, pg_ref, cot_ref, wt_ref, fwd_ref, bwd_ref,
    twg_ref, dwt_ref, gb_ref, mf, dm, dw, prs,
):
    parts, count, width, lanes = wt_ref.shape
    step = pl.program_id(0)
    depth = cot_ref.shape[0]
    tile = min(256, depth)
    order = [order_ref[a] for a in range(parts)]

    def columns(a):
        return slice(a * lanes, (a + 1) * lanes)

    @pl.when(step == 0)
    def _():
        @pl.loop(0, count)
        def _(f):
            rows = jnp.concatenate([wt_ref[order[a], f] for a in range(parts)], axis=1)
            both = jnp.dot(fwd_ref[...], rows, preferred_element_type=jnp.float32)
            value = both[:width] + both[width:]
            for a in range(parts):
                mf[a, f] = value[:, columns(a)]
                dm[a, f] = jnp.zeros((width, lanes), jnp.float32)
                dw[a, f] = jnp.zeros((width, lanes), jnp.float32)

    @pl.loop(0, chunk)
    def _(q):
        i = left_ref[step * chunk + q]
        j = right_ref[step * chunk + q]
        rows = pl.ds(pl.multiple_of(q * width, width), width)
        for a in range(parts):
            g = pg_ref[rows, columns(a)].astype(jnp.float32)
            w = wt_ref[order[a], j].astype(jnp.float32)
            m = mf[a, i]
            prs[rows, columns(a)] = (m * w).astype(jnp.bfloat16)
            dm[a, i] += g * w
            dw[a, j] += g * m

    @pl.loop(0, depth // tile)
    def _(c):
        cols = pl.ds(pl.multiple_of(c * tile, tile), tile)
        twg_ref[:, cols] = lax.dot_general(
            prs[...], cot_ref[cols, :], (((1,), (1,)), ((), ())), preferred_element_type=jnp.float32
        ).astype(jnp.bfloat16)

    @pl.when(step == pl.num_programs(0) - 1)
    def _():
        gb_ref[...] = jnp.zeros_like(gb_ref)

        @pl.loop(0, count)
        def _(f):
            d = jnp.concatenate([dm[a, f].astype(jnp.bfloat16) for a in range(parts)], axis=1)
            rows = jnp.concatenate([wt_ref[order[a], f] for a in range(parts)], axis=1)
            both = jnp.dot(bwd_ref[...], d, preferred_element_type=jnp.float32)
            value = both[:width] + both[width:]
            for a in range(parts):
                dwt_ref[order[a], f] = (dw[a, f] + value[:, columns(a)]).astype(jnp.bfloat16)
            gb_ref[...] += lax.dot_general(
                rows, d, (((1,), (1,)), ((), ())), preferred_element_type=jnp.float32
            )


def two_parts(matrix):
    top = matrix.astype(jnp.bfloat16)
    rest = (matrix - top.astype(jnp.float32)).astype(jnp.bfloat16)
    return jnp.concatenate([top, rest], axis=0)


def tower_step(left, right, order, pair_grad, cot, weighted, w_bilinear):
    parts, count, width, lanes = weighted.shape
    depth = cot.shape[0]
    pairs = left.shape[0]
    steps = next(c for c in (3, 2, 4, 5, 6, 7, 1) if pairs % c == 0)
    chunk = pairs // steps
    rows = chunk * width
    samples = parts * lanes

    def whole(shape):
        return pl.BlockSpec(shape, lambda s, *_: (0,) * len(shape), pipeline_mode=pl.Buffered(1))

    big = (parts, count, width, lanes)
    return pl.pallas_call(
        functools.partial(tower_kernel, chunk),
        grid_spec=pltpu.PrefetchScalarGridSpec(
            num_scalar_prefetch=3,
            grid=(steps,),
            in_specs=[
                pl.BlockSpec((rows, samples), lambda s, *_: (s, 0)),
                whole(cot.shape),
                whole(big),
                whole((2 * width, width)),
                whole((2 * width, width)),
            ],
            out_specs=[
                pl.BlockSpec((rows, depth), lambda s, *_: (s, 0)),
                whole(big),
                whole((width, width)),
            ],
            scratch_shapes=[
                pltpu.VMEM(big, jnp.float32),
                pltpu.VMEM(big, jnp.float32),
                pltpu.VMEM(big, jnp.float32),
                pltpu.VMEM((rows, samples), jnp.bfloat16),
            ],
        ),
        out_shape=[
            jax.ShapeDtypeStruct((pairs * width, depth), jnp.bfloat16),
            jax.ShapeDtypeStruct(big, jnp.bfloat16),
            jax.ShapeDtypeStruct((width, width), jnp.float32),
        ],
        compiler_params=pltpu.CompilerParams(
            dimension_semantics=("arbitrary",), vmem_limit_bytes=60 * 1024 * 1024
        ),
        cost_estimate=pl.CostEstimate(
            flops=2 * pairs * width * depth * samples,
            bytes_accessed=4 * pairs * width * depth,
            transcendentals=0,
        ),
    )(left, right, order, pair_grad, cot, weighted, two_parts(w_bilinear.T), two_parts(w_bilinear))


def on_device(pooled, field_owner, w_squeeze, w_excite, w_bilinear, tower_weight, tower_cotangent):
    per_owner, width, samples = pooled.shape[0], pooled.shape[3], pooled.shape[4]
    count = field_owner.shape[0]
    hidden = w_squeeze.shape[0]
    parts, locals_, subs = lax.axis_size("a"), lax.axis_size("l"), lax.axis_size("sub")
    tables = parts * locals_
    size = locals_ * subs
    me = lax.axis_index("l") * subs + lax.axis_index("sub")
    scale = 1.0 / width**0.5
    signs = hadamard_table(width)

    rotated = (
        jnp.einsum("ij,ktsjb->ktsib", signs, pooled, preferred_element_type=jnp.float32) * scale
    ).astype(jnp.bfloat16)
    received = lax.all_to_all(rotated, TABLE, split_axis=1, concat_axis=0, tiled=True)
    received = received.reshape(per_owner * tables, width, samples)
    slot_index = slot_table(field_owner, per_owner)
    selected = jnp.take(received, slot_index, axis=0)
    fields = jnp.einsum("ij,fjn->fin", signs, selected, preferred_element_type=jnp.float32) * scale
    squeezed = jnp.mean(fields, axis=1)
    raw = jnp.dot(w_squeeze, squeezed, precision=HIGH)
    gate = jax.nn.sigmoid(raw)
    activated = raw * gate
    excite = jnp.dot(w_excite, activated, precision=HIGH).reshape(count, width, samples)
    weighted = fields * (1.0 + excite)
    narrow = weighted.astype(jnp.bfloat16)
    weighted_all = lax.all_gather(narrow, "a", axis=0, tiled=False)

    mine_a = lax.axis_index("a")
    order = jnp.arange(parts, dtype=jnp.int32) ^ mine_a
    rows = tower_weight.shape[0]
    cot = jnp.concatenate(spread(tower_cotangent, "a", parts, narrow), axis=1)
    shards = spread(tower_weight, GROUP, size, narrow)
    pair_grad = jnp.zeros((size * rows, parts * samples), jnp.bfloat16)
    for offset, shard in enumerate(shards):
        block = jnp.dot(shard, cot, preferred_element_type=jnp.float32).astype(jnp.bfloat16)
        pair_grad = lax.dynamic_update_slice_in_dim(pair_grad, block, (me ^ offset) * rows, 0)

    table_left, table_right = np.triu_indices(count, 1)
    mine = table_left.shape[0] // parts
    start = mine_a * mine
    left = lax.dynamic_slice_in_dim(jnp.asarray(table_left, jnp.int32), start, mine)
    right = lax.dynamic_slice_in_dim(jnp.asarray(table_right, jnp.int32), start, mine)
    totals, partial, d_bilinear = tower_step(
        left, right, order, pair_grad, cot, weighted_all, w_bilinear
    )

    arrived = lax.all_to_all(partial, "a", split_axis=0, concat_axis=0, tiled=True)
    d_weighted = jnp.sum(arrived.astype(jnp.float32), axis=0)
    weight_total = scatter_rows(totals, size, me)

    d_excite = (d_weighted * fields).reshape(count * width, samples)
    g_excite = lax.dot_general(activated, d_excite, (((1,), (1,)), ((), ())), precision=HIGH)
    d_act = lax.dot_general(w_excite, d_excite, (((0,), (0,)), ((), ())), precision=HIGH)
    d_raw = d_act * (gate * (1.0 + raw * (1.0 - gate)))
    g_squeeze = lax.dot_general(d_raw, squeezed, (((1,), (1,)), ((), ())), precision=HIGH)
    d_squeezed = lax.dot_general(w_squeeze, d_raw, (((0,), (0,)), ((), ())), precision=HIGH)
    field_grad = d_weighted * (1.0 + excite) + (d_squeezed * (1.0 / width))[:, None, :]

    slot_count = per_owner * tables
    onehot = (slot_index[None, :] == jnp.arange(slot_count, dtype=jnp.int32)[:, None]).astype(
        jnp.bfloat16
    )
    placed = jnp.einsum(
        "sf,fen->sen", onehot, field_grad.astype(jnp.bfloat16), preferred_element_type=jnp.float32
    ).astype(jnp.bfloat16)
    placed = placed.reshape(slot_count, 1, 1, width, samples)
    row_grads = lax.all_to_all(placed, TABLE, split_axis=0, concat_axis=1, tiled=True)

    flat = jnp.concatenate([g_excite.reshape(-1), g_squeeze.reshape(-1), d_bilinear.reshape(-1)])
    devices = tables * subs
    inverse = 1.0 / (devices * samples)
    devices = tables * subs
    inverse = 1.0 / (devices * samples)
    flat = jnp.pad(flat, (0, -flat.shape[0] % 1024)).reshape(-1, 128) * inverse
    flat = lax.optimization_barrier((flat, placed))[0]
    for bit in bits_of(devices):
        flat = flat + lax.ppermute(flat, EVERY, [(d, d ^ bit) for d in range(devices)])
    flat = flat.reshape(-1)
    n_excite, n_squeeze = count * width * hidden, hidden * count
    g_excite = flat[:n_excite].reshape(hidden, count * width).T
    g_squeeze = flat[n_excite : n_excite + n_squeeze].reshape(hidden, count)
    at = n_excite + n_squeeze
    g_bilinear = flat[at : at + width * width].reshape(width, width)
    return (row_grads, weight_total * inverse, g_squeeze, g_excite, g_bilinear)


def solution(mesh):
    tables, subs = mesh.shape["table"], mesh.shape["sub"]

    def run(pooled, field_owner, *rest):
        count = field_owner.shape[0]
        pairs = count * (count - 1) // 2
        parts = max(a for a in range(1, tables + 1) if tables % a == 0 and pairs % a == 0)
        fine = Mesh(mesh.devices.reshape(parts, tables // parts, subs), EVERY)
        return jax.shard_map(
            on_device,
            mesh=fine,
            in_specs=(
                P(TABLE, None, "sub", None, None),
                P(),
                P(),
                P(),
                P(),
                P(EVERY, None),
                P(None, EVERY),
            ),
            out_specs=(P(TABLE, None, "sub", None, None), P(EVERY, None), P(), P(), P()),
            check_vma=False,
        )(pooled, field_owner, *rest)

    return run
```
